128 devices in a mesh: ma: 4 (over y), af: 32 (over x, z, core).
Axes of the slice: x: 4, y: 4, z: 4, core: 2. Of those that a mesh axis runs over, the one named last changes fastest.
Arguments:
- beams: bfloat16 [4, 32, 4, 512, 2048], P(None, 'af', 'ma'), may hold values from -2 to 2
- spectrum: float32 [128, 3, 1024], P('af'), may hold values from 0.3 to 3
- partners: int32 [128, 3], P('af'), may hold values from 0 to 127, as said below
Outputs:
- covariance: bfloat16 [4, 128, 3, 2, 512, 512], P('ma', 'af')
The draws below stay inside these ranges and needn't reach their ends.
Inputs may be any that keep to these rules, and one draw needn't show every extreme that they name: partners[c, k] lies in the band of c (channels 64 * (c // 64) up to the band's end or the last channel) and at most 2 channels from c; the distance 2 occurs.
All inputs are finite; a program needn't handle non-finite values.
Results may differ from the reference program's by a relative error of at most 0.0044.
Values may be sent and summed in bfloat16 or wider, within the bound.
No kernel may reach another device: no remote copies, remote signals or barrier semaphores. Data moves between devices by JAX's collectives and lax.ppermute only.
A program may use at most 192 MiB of HBM per device.

```python
import math
import jax
import jax.numpy as jnp
from jax import lax

NB = 512
NL = 1024
FL = 4
K = 3
REACH = 2
BAND = 64
M = 4
FH = 32
F = 128


def draw_partners(key, part):
    key = jax.random.fold_in(key, 7)
    channel = jnp.arange(F, dtype=jnp.int32)[:, None]
    offsets = jax.random.randint(key, (F, K), -REACH, REACH + 1, dtype=jnp.int32)
    lower = channel // BAND * BAND
    upper = jnp.minimum(lower + BAND, F) - 1
    chosen = jnp.clip(channel + offsets, lower, upper)
    chosen = chosen.at[0, K - 1].set(REACH)
    chosen = chosen.at[0, 0].set(0)
    chosen = chosen.at[F - 1, 0].set(F - 1)
    return chosen


def block_scale(key, shape, split, low, top_value):
    def one(dim, parts):
        draws = jax.random.uniform(jax.random.fold_in(jax.random.fold_in(key, 6), dim), (parts,), jnp.float32, low / len(split), top_value / len(split))
        return jnp.repeat(jnp.exp(draws), shape[dim] // parts).reshape((-1,) + (1,) * (len(shape) - dim - 1))

    gain = one(*split[0])
    for cut in split[1:]:
        gain = gain * one(*cut)
    return gain


def bell_draw(rng, dims, width, limit, split=(), kind=jnp.bfloat16):
    result = width * jax.random.normal(rng, dims, jnp.float32)
    if split:
        result = result * block_scale(rng, dims, split, -0.22, 0.18)
    return jnp.clip(result, -limit, limit).astype(kind)


def setup_inputs(seed: int = 0) -> dict:
    seeds = jax.random.split(jax.random.key(seed), 4)
    beams = bell_draw(seeds[0], (M, FH, FL, NB, 2 * NL), ((2 * NL) ** -0.25), 2.0, ((1, 32), (2, 4)))
    spectrum = jnp.clip(jnp.exp(math.log(3.0) - 2.3025851 * jax.random.uniform(seeds[1], (F, K, NL), jnp.float32) ** block_scale(seeds[1], (F, K, NL), ((0, 32),), -0.2, 0.2)), 0.3, 3.0)
    partners = draw_partners(jax.random.fold_in(seeds[3], 71), 0)
    return dict(beams=beams, spectrum=spectrum, partners=partners)


def sandwich(own, right, weights):
    half = own.shape[-1] // 2
    real_part = own[:, :half].astype(jnp.float32) * weights
    imag_part = own[:, half:].astype(jnp.float32) * weights
    upper = jnp.concatenate([real_part, imag_part], axis=1)
    lower = jnp.concatenate([imag_part, -real_part], axis=1)
    left = jnp.concatenate([upper, lower], axis=0).astype(jnp.bfloat16)
    product = jnp.dot(left, right.T, preferred_element_type=jnp.float32)
    return product.astype(jnp.bfloat16).reshape(2, own.shape[0], own.shape[0])


def reference(beams, spectrum, partners):
    flat = beams.reshape(M, F, NB, 2 * NL)
    results = []
    for mval in range(M):
        blocks = flat[mval]

        def one_channel(channel):
            own = lax.dynamic_index_in_dim(blocks, channel, 0, keepdims=False)
            weights = lax.dynamic_index_in_dim(spectrum, channel, 0, keepdims=False)
            targets = lax.dynamic_index_in_dim(partners, channel, 0, keepdims=False)
            outs = []
            for slot in range(K):
                right = lax.dynamic_index_in_dim(blocks, targets[slot].astype(jnp.int32), 0, keepdims=False)
                outs.append(sandwich(own, right, weights[slot]))
            return jnp.stack(outs, axis=0)

        results.append(lax.map(one_channel, jnp.arange(F, dtype=jnp.int32)))
    return jnp.stack(results, axis=0)
```

```python
import functools

import jax
import jax.numpy as jnp
from jax import lax
from jax.experimental import pallas as pl
from jax.experimental.pallas import tpu as pltpu
from jax.sharding import PartitionSpec as P

BAND = 64
HALF = 256
LATE = 2
VMEM = 60 * 2**20
NT = (((1,), (1,)), ((), ()))
ORDER = lax.optimization_barrier


def plan_kernel(stages, caps, partners, *refs):
    lists, loads = refs[:stages], refs[stages]
    chans, slots = partners.shape
    last = 2 * chans * slots
    pos = lax.axis_index("ma")
    group = lax.axis_index("af")
    for stage in range(stages):
        lists[stage][last, 0] = 0
        loads[stage] = 0

    def put(when, stage, kind, half, channel, slot, own, source):
        @pl.when(when)
        def _():
            jobs = lists[stage - 1]
            count = jobs[last, 0]
            own_part = 1 << half if kind == 0 else 3
            source_part = 1 << half if kind == 1 else 3
            mask = jnp.left_shift(own_part, own * 2) | jnp.left_shift(source_part, source * 2)
            for place, field in enumerate((kind, half, channel, slot, own, source, mask)):
                jobs[count, place] = field
            jobs[last, 0] = count + 1
            loads[stage - 1] = loads[stage - 1] + (2 if kind == 2 else 1)

    def visit(late):
        def one(index, carry):
            channel = lax.div(index, slots)
            slot = lax.rem(index, slots)
            offset = partners[channel, slot] - group * chans
            own = lax.rem(channel - pos + 4, 4)
            partner = lax.rem(offset - pos + 8, 4)
            outside = jnp.logical_or(offset < 0, offset >= chans)
            inside = jnp.logical_not(outside)
            source = jnp.where(outside, partner + 4, partner)
            own_late, own_early = own == LATE, own != LATE
            other_late, other_early = partner == LATE, partner != LATE
            soon = jnp.logical_or(inside, partner == 0)
            plain = own_early & other_early
            names = dict(channel=channel, slot=slot, own=own, source=source)
            if late:
                put(own_late & other_early, 2, 0, 0, **names)
                put(own_early & other_late & inside, 2, 1, 0, **names)
                put(own_late & jnp.logical_or(other_early, inside), 3, 0, 1, **names)
                put(own_late & other_late & inside, 3, 0, 0, **names)
                put(own_early & other_late & inside, 3, 1, 1, **names)
                put(own_early & other_late & outside, 3, 1, 0, **names)
                put(own_early & other_late & outside, 4, 1, 1, **names)
            else:
                room = loads[0] < caps[0]
                put(plain & soon & room, 1, 2, 0, **names)
                room = jnp.logical_and(soon, room)
                fits = loads[1] < caps[1]
                put(plain & jnp.logical_not(room) & fits, 2, 2, 0, **names)
                put(plain & jnp.logical_not(room) & jnp.logical_not(fits), 3, 2, 0, **names)
            return carry

        lax.fori_loop(0, chans * slots, one, 0)

    visit(True)
    visit(False)


def make_plan(partners, caps):
    chans, slots = partners.shape
    stages = 4
    scalars = pl.BlockSpec(memory_space=pltpu.SMEM)
    return pl.pallas_call(
        functools.partial(plan_kernel, stages, caps),
        out_shape=[jax.ShapeDtypeStruct((2 * chans * slots + 1, 7), jnp.int32)] * stages,
        in_specs=[scalars],
        out_specs=[scalars] * stages,
        scratch_shapes=[pltpu.SMEM((stages,), jnp.int32)],
        cost_estimate=pl.CostEstimate(flops=1, bytes_accessed=1, transcendentals=0),
        name="plan",
    )(partners)


def kernel(kinds, names, *refs):
    jobs, spectrum = refs[:2]
    pieces = dict(zip(names, refs[2 : 2 + len(names)]))
    out, state, held, rows_out, columns_out, whole_out, in_sems, out_sems = refs[-8:]
    outs = (rows_out, columns_out, whole_out)
    pos = lax.axis_index("ma")
    total = jobs[jobs.shape[0] - 1, 0]
    state[0] = 0
    state[1] = 0

    def fills(part):
        source, half = part // 2, part % 2
        copies = []
        for (name, first), ref in pieces.items():
            if name != source:
                continue
            if name == 0:
                copies.append((ref.at[pos, pl.ds(half * HALF, HALF)], held.at[part]))
                continue
            height = ref.shape[0]
            low = max(first, half * HALF)
            high = min(first + height, half * HALF + HALF)
            if low < high:
                view = ref.at[pl.ds(low - first, high - low)]
                copies.append((view, held.at[part, pl.ds(low - half * HALF, high - low)]))
        return copies

    def each(mask, act):
        @pl.when(mask != 0)
        def _():
            for part in range(16):
                places = fills(part)
                if places:

                    @pl.when(jnp.bitwise_and(mask, 1 << part) != 0)
                    def _():
                        for place in places:
                            act(pltpu.make_async_copy(*place, in_sems.at[part]))

    def fetch(job):
        mask = jobs[job, 6] & ~state[0]
        each(mask, lambda copy: copy.start())
        state[0] = state[0] | mask

    def arrive(job):
        mask = jobs[job, 6] & ~state[1]
        each(mask, lambda copy: copy.wait())
        state[1] = state[1] | mask

    def scaled(block, weights):
        block = block.astype(jnp.float32)
        width = weights.shape[-1]
        real = (block[:, :width] * weights).astype(jnp.bfloat16)
        imag = (block[:, width:] * weights).astype(jnp.bfloat16)
        upper = jnp.concatenate([real, imag], axis=1)
        lower = jnp.concatenate([imag, -real], axis=1)
        return jnp.concatenate([upper, lower], axis=0)

    def write(kind, job, place):
        target = out.at[jobs[job, 2], jobs[job, 3]]
        some = pl.ds(pl.multiple_of(jobs[job, 1] * HALF, HALF), HALF)
        if kind == 0:
            target = target.at[:, some, :]
        if kind == 1:
            target = target.at[:, :, some]
        return pltpu.make_async_copy(outs[kind].at[place], target, out_sems.at[place])

    def drain(job):
        for kind in kinds:

            @pl.when(jobs[job, 0] == kind)
            def _():
                write(kind, job, lax.rem(job, 2)).wait()

    @pl.when(total > 0)
    def _():
        fetch(0)

    def step(job, carry):
        place = lax.rem(job, 2)
        half, own, partner = jobs[job, 1], jobs[job, 4], jobs[job, 5]
        arrive(job)

        @pl.when(job + 1 < total)
        def _():
            fetch(job + 1)

        @pl.when(job >= 2)
        def _():
            drain(job - 2)

        weights = spectrum[jobs[job, 2], pl.ds(jobs[job, 3], 1), :]

        def taken(source, whole):
            if not whole:
                return held[source * 2 + half]
            block = held[pl.ds(source * 2, 2)]
            return block.reshape(2 * HALF, block.shape[2])

        for kind in kinds:

            @pl.when(jobs[job, 0] == kind)
            def _():
                left = scaled(taken(own, kind != 0), weights)
                right = taken(partner, kind != 1)
                product = lax.dot_general(left, right, NT, preferred_element_type=jnp.float32)
                outs[kind][place] = product.astype(jnp.bfloat16).reshape(outs[kind].shape[1:])
                write(kind, job, place).start()

        return carry

    lax.fori_loop(0, total, step, 0)

    @pl.when(total >= 2)
    def _():
        drain(total - 2)

    @pl.when(total >= 1)
    def _():
        drain(total - 1)


def run_stage(name, kinds, jobs, spectrum, pieces, out, weight):
    chans, slots, _ = spectrum.shape
    names = tuple(pieces)
    arrays = [pieces[name] for name in names]
    rows, width = arrays[0].shape[-2:]
    whole = pl.BlockSpec(memory_space=pl.ANY)
    operands = [jobs, spectrum, *arrays]
    specs = [pl.BlockSpec(memory_space=pltpu.SMEM), pl.BlockSpec(memory_space=pltpu.VMEM)] + [whole] * len(arrays)
    aliases = {}
    if out is not None:
        aliases = {len(operands): 0}
        operands.append(out)
        specs.append(whole)
    return pl.pallas_call(
        functools.partial(kernel, kinds, names),
        out_shape=jax.ShapeDtypeStruct((chans, slots, 2, rows, rows), jnp.bfloat16),
        in_specs=specs,
        out_specs=whole,
        input_output_aliases=aliases,
        scratch_shapes=[
            pltpu.SMEM((2,), jnp.int32),
            pltpu.VMEM((16, HALF, width), jnp.bfloat16),
            pltpu.VMEM((2, 2, HALF, rows), jnp.bfloat16),
            pltpu.VMEM((2, 2, rows, HALF), jnp.bfloat16),
            pltpu.VMEM((2, 2, rows, rows), jnp.bfloat16),
            pltpu.SemaphoreType.DMA((16,)),
            pltpu.SemaphoreType.DMA((2,)),
        ],
        compiler_params=pltpu.CompilerParams(vmem_limit_bytes=VMEM),
        cost_estimate=pl.CostEstimate(flops=weight, bytes_accessed=weight, transcendentals=0),
        name=name,
    )(*operands)


def cut_kernel(shift, cuts, step, beams, *refs):
    outs, (held, in_sems, out_sems) = refs[: len(cuts)], refs[len(cuts) :]
    which = lax.rem(lax.axis_index("ma") + shift, lax.axis_size("ma"))
    inward, outward = [], []
    for (first, height), out in zip(cuts, outs):
        for row in range(0, height, step):
            part = len(inward)
            source = beams.at[which, pl.ds(first + row, step)]
            inward.append(pltpu.make_async_copy(source, held.at[part], in_sems.at[part]))
            outward.append(pltpu.make_async_copy(held.at[part], out.at[pl.ds(row, step)], out_sems.at[part]))
    for copy in inward:
        copy.start()
    for there, back in zip(inward, outward):
        there.wait()
        back.start()
    for copy in outward:
        copy.wait()


def cut_out(beams, shift, *cuts):
    step = 64
    parts = sum(height for _, height in cuts) // step
    whole = pl.BlockSpec(memory_space=pl.ANY)
    return pl.pallas_call(
        functools.partial(cut_kernel, shift, cuts, step),
        out_shape=[jax.ShapeDtypeStruct((height, beams.shape[2]), beams.dtype) for _, height in cuts],
        in_specs=[whole],
        out_specs=[whole] * len(cuts),
        scratch_shapes=[
            pltpu.VMEM((parts, step, beams.shape[2]), beams.dtype),
            pltpu.SemaphoreType.DMA((parts,)),
            pltpu.SemaphoreType.DMA((parts,)),
        ],
        compiler_params=pltpu.CompilerParams(vmem_limit_bytes=VMEM),
        cost_estimate=pl.CostEstimate(flops=10**12, bytes_accessed=1, transcendentals=0),
        name=f"cut{shift}",
    )(beams)


def along(array, by):
    count = lax.axis_size("ma")
    return lax.ppermute(array, "ma", [(i, (i + by) % count) for i in range(count)])


def beside(array, source, per_band):
    many, groups = lax.axis_size("ma"), lax.axis_size("af")
    pairs = []
    for pos in range(many):
        for group in range(groups):
            channel = (pos + source) % many
            target = group + 1 if channel >= many // 2 else group - 1
            if 0 <= target < groups and target // per_band == group // per_band:
                pairs.append((pos * groups + group, pos * groups + target))
    return lax.ppermute(array, ("ma", "af"), pairs)


def body(beams, spectrum, partners):
    many, _, _, rows, width = beams.shape
    per_band = BAND // many
    beams = beams.reshape(many, rows, width)
    cuts = [(0, 64), (64, 256), (320, 192)]

    (downward,) = cut_out(beams, 3, (0, rows))
    (upward,) = cut_out(beams, 1, (0, rows))
    (own,) = cut_out(beams, 0, (0, rows))
    (far0,) = cut_out(beams, 2, cuts[0])
    far1, far2 = cut_out(beams, 2, *cuts[1:])
    plan = make_plan(partners, (12, 10))

    near3 = along(upward, 1)
    near1 = along(downward, -1)
    side0 = beside(own, 0, per_band)
    late0 = along(far0, 2)
    far1, far2, near1, near3 = ORDER((far1, far2, near1, near3))
    late1 = along(far1, 2)
    late2 = along(far2, 2)
    side1 = beside(near1, 1, per_band)
    side3 = beside(near3, 3, per_band)

    side0, late0 = ORDER((side0, late0))
    pieces = {(0, 0): beams, (1, 0): near1, (3, 0): near3, (4, 0): side0}
    out = run_stage("early", (2,), plan[0], spectrum, pieces, None, 6 * 10**12)

    first, out = ORDER((jnp.concatenate([late0, late1], axis=0), out))
    side_first = beside(first, 2, per_band)
    pieces = pieces | {(5, 0): side1, (7, 0): side3, (2, 0): first}
    out = run_stage("middle", (0, 1, 2), plan[1], spectrum, pieces, out, 0)

    late2, out = ORDER((late2, out))
    side_second = beside(late2, 2, per_band)
    side_first, out = ORDER((side_first, out))
    pieces = pieces | {(2, 320): late2, (6, 0): side_first}
    out = run_stage("late", (0, 1, 2), plan[2], spectrum, pieces, out, 0)

    side_second, out = ORDER((side_second, out))
    pieces = {(0, 0): beams, (1, 0): near1, (3, 0): near3, (6, 0): side_first, (6, 320): side_second}
    out = run_stage("last", (1,), plan[3], spectrum, pieces, out, 0)
    return out[None]


def solution(mesh):
    in_specs = (P(None, "af", "ma", None, None), P("af", None, None), P("af", None))
    out_specs = P("ma", "af", None, None, None, None)
    return jax.shard_map(body, mesh=mesh, in_specs=in_specs, out_specs=out_specs, check_vma=False)
```

```python
import functools

import jax
import jax.numpy as jnp
from jax import lax
from jax.experimental import pallas as pl
from jax.experimental.pallas import tpu as pltpu
from jax.sharding import PartitionSpec as P

BAND = 64
HALF = 256
LATE = 2
VMEM = 56 * 2**20
STAGE_VMEM = 47 * 2**20
CAPS = (9, 8)
FIRST_ROWS = 256
WEIGHTS = (10**12, 0, 0, 0)
NT = (((1,), (1,)), ((), ()))
ORDER = lax.optimization_barrier


def plan_kernel(stages, caps, partners, *refs):
    lists, loads = refs[:stages], refs[stages]
    chans, slots = partners.shape
    last = 2 * chans * slots
    pos = lax.axis_index("ma")
    group = lax.axis_index("af")
    for stage in range(stages):
        lists[stage][last, 0] = 0
        loads[stage] = 0

    def put(when, stage, kind, half, channel, slot, own, source):
        @pl.when(when)
        def _():
            jobs = lists[stage - 1]
            count = jobs[last, 0]
            own_part = 1 << half if kind == 0 else 3
            source_part = 1 << half if kind == 1 else 3
            mask = jnp.left_shift(own_part, own * 2) | jnp.left_shift(source_part, source * 2)
            for place, field in enumerate((kind, half, channel, slot, own, source, mask)):
                jobs[count, place] = field
            jobs[last, 0] = count + 1
            loads[stage - 1] = loads[stage - 1] + (2 if kind == 2 else 1)

    def visit(late):
        def one(index, carry):
            channel = lax.div(index, slots)
            slot = lax.rem(index, slots)
            offset = partners[channel, slot] - group * chans
            own = lax.rem(channel - pos + 4, 4)
            partner = lax.rem(offset - pos + 8, 4)
            outside = jnp.logical_or(offset < 0, offset >= chans)
            inside = jnp.logical_not(outside)
            source = jnp.where(outside, partner + 4, partner)
            own_late, own_early = own == LATE, own != LATE
            other_late, other_early = partner == LATE, partner != LATE
            early = jnp.logical_or(inside, partner == 0)
            plain = own_early & other_early
            names = dict(channel=channel, slot=slot, own=own, source=source)
            if late:
                put(own_late & other_early, 2, 0, 0, **names)
                put(own_early & other_late & inside, 2, 1, 0, **names)
                put(own_late & other_early, 3, 0, 1, **names)
                put(own_late & other_late & inside, 3, 2, 0, **names)
                put(own_early & other_late & inside, 3, 1, 1, **names)
                put(own_early & other_late & outside, 3, 1, 0, **names)
                put(own_early & other_late & outside, 4, 1, 1, **names)
            else:
                left = plain
                for stage, may in ((1, early), (2, True)):
                    fits = jnp.logical_and(loads[stage - 1] < caps[stage - 1], may)
                    put(left & fits, stage, 2, 0, **names)
                    left = left & jnp.logical_not(fits)
                put(left, 3, 2, 0, **names)
            return carry

        lax.fori_loop(0, chans * slots, one, 0)

    visit(True)
    visit(False)


def make_plan(partners, caps):
    chans, slots = partners.shape
    stages = 4
    scalars = pl.BlockSpec(memory_space=pltpu.SMEM)
    return pl.pallas_call(
        functools.partial(plan_kernel, stages, caps),
        out_shape=[jax.ShapeDtypeStruct((2 * chans * slots + 1, 7), jnp.int32)] * stages,
        in_specs=[scalars],
        out_specs=[scalars] * stages,
        scratch_shapes=[pltpu.SMEM((stages,), jnp.int32)],
        cost_estimate=pl.CostEstimate(flops=10**12, bytes_accessed=1, transcendentals=0),
        name="plan",
    )(partners)


def kernel(kinds, names, ready, fill, keep, *refs):
    jobs, spectrum = refs[:2]
    pieces = dict(zip(names, refs[2 : 2 + len(names)]))
    out, held, state, rows_out, columns_out, whole_out, in_sems, out_sems = refs[-8:]
    outs = (rows_out, columns_out, whole_out)
    pos = lax.axis_index("ma")
    total = jobs[jobs.shape[0] - 1, 0]

    places = {}
    for (source, first), ref in pieces.items():
        if source == 0:
            ref = ref.at[pos]
        for half in range(2):
            low, high = max(first, half * HALF), min(first + ref.shape[0], half * HALF + HALF)
            if low < high and source * 2 + half in fill:
                into = held.at[source * 2 + half, pl.ds(low - half * HALF, high - low)]
                places.setdefault(source * 2 + half, []).append((ref.at[pl.ds(low - first, high - low)], into))
    fresh = sum(1 << part for part in places)
    state[0] = ready
    state[1] = ready

    def each(mask, act):
        @pl.when(mask != 0)
        def _():
            for part, copies in places.items():

                @pl.when(jnp.bitwise_and(mask, 1 << part) != 0)
                def _():
                    for copy in copies:
                        act(pltpu.make_async_copy(*copy, in_sems.at[part]))

    def fetch(wanted):
        mask = wanted & ~state[0]
        each(mask, lambda copy: copy.start())
        state[0] = state[0] | mask

    def arrive(wanted):
        mask = wanted & ~state[1]
        each(mask, lambda copy: copy.wait())
        state[1] = state[1] | mask

    def scaled(block, weights):
        block = block.astype(jnp.float32)
        width = weights.shape[-1]
        real = (block[:, :width] * weights).astype(jnp.bfloat16)
        imag = (block[:, width:] * weights).astype(jnp.bfloat16)
        upper = jnp.concatenate([real, imag], axis=1)
        lower = jnp.concatenate([imag, -real], axis=1)
        return jnp.concatenate([upper, lower], axis=0)

    def write(kind, job, place):
        target = out.at[jobs[job, 2], jobs[job, 3]]
        some = pl.ds(pl.multiple_of(jobs[job, 1] * HALF, HALF), HALF)
        if kind == 0:
            target = target.at[:, some, :]
        if kind == 1:
            target = target.at[:, :, some]
        return pltpu.make_async_copy(outs[kind].at[place], target, out_sems.at[place])

    def drain(job):
        for kind in kinds:

            @pl.when(jobs[job, 0] == kind)
            def _():
                write(kind, job, lax.rem(job, 2)).wait()

    @pl.when(total > 0)
    def _():
        fetch(jobs[0, 6])

    if keep:
        fetch(jnp.int32(fresh))

    def step(job, carry):
        place = lax.rem(job, 2)
        half, own, partner = jobs[job, 1], jobs[job, 4], jobs[job, 5]
        arrive(jobs[job, 6])
        if not keep:

            @pl.when(job + 1 < total)
            def _():
                fetch(jobs[job + 1, 6])

        @pl.when(job >= 2)
        def _():
            drain(job - 2)

        weights = spectrum[jobs[job, 2], pl.ds(jobs[job, 3], 1), :]

        def taken(source, whole):
            if not whole:
                return held[source * 2 + half]
            block = held[pl.ds(source * 2, 2)]
            return block.reshape(2 * HALF, block.shape[2])

        for kind in kinds:

            @pl.when(jobs[job, 0] == kind)
            def _():
                left = scaled(taken(own, kind != 0), weights)
                right = taken(partner, kind != 1)
                product = lax.dot_general(left, right, NT, preferred_element_type=jnp.float32)
                outs[kind][place] = product.astype(jnp.bfloat16).reshape(outs[kind].shape[1:])
                write(kind, job, place).start()

        return carry

    lax.fori_loop(0, total, step, 0)
    if keep:
        arrive(jnp.int32(fresh))

    @pl.when(total >= 2)
    def _():
        drain(total - 2)

    @pl.when(total >= 1)
    def _():
        drain(total - 1)


def run_stage(name, kinds, jobs, spectrum, pieces, ready, fill, held, out, weight):
    chans, slots, _ = spectrum.shape
    names = tuple(pieces)
    arrays = [pieces[name] for name in names]
    rows, width = 2 * HALF, arrays[0].shape[-1]
    whole = pl.BlockSpec(memory_space=pl.ANY)
    vector = pl.BlockSpec(memory_space=pltpu.VMEM)
    operands = [jobs, spectrum, *arrays]
    specs = [pl.BlockSpec(memory_space=pltpu.SMEM), vector] + [whole] * len(arrays)
    aliases = {}
    if out is not None:
        aliases = {len(operands): 0, len(operands) + 1: 1}
        operands += [out, held]
        specs += [whole, vector]
    return pl.pallas_call(
        functools.partial(kernel, kinds, names, sum(1 << part for part in ready), fill, name != "last"),
        out_shape=[
            jax.ShapeDtypeStruct((chans, slots, 2, rows, rows), jnp.bfloat16),
            pltpu.VMEM((16, HALF, width), jnp.bfloat16),
        ],
        in_specs=specs,
        out_specs=[whole, vector],
        input_output_aliases=aliases,
        scratch_shapes=[
            pltpu.SMEM((2,), jnp.int32),
            pltpu.VMEM((2, 2, HALF, rows), jnp.bfloat16),
            pltpu.VMEM((2, 2, rows, HALF), jnp.bfloat16),
            pltpu.VMEM((2, 2, rows, rows), jnp.bfloat16),
            pltpu.SemaphoreType.DMA((16,)),
            pltpu.SemaphoreType.DMA((2,)),
        ],
        compiler_params=pltpu.CompilerParams(vmem_limit_bytes=STAGE_VMEM),
        cost_estimate=pl.CostEstimate(flops=weight, bytes_accessed=weight, transcendentals=0),
        name=name,
    )(*operands)


def cut_kernel(cuts, step, beams, *refs):
    outs, (held, in_sems, out_sems) = refs[: len(cuts)], refs[len(cuts) :]
    pos, many = lax.axis_index("ma"), lax.axis_size("ma")
    inward, outward = [], []
    for (shift, first, height), out in zip(cuts, outs):
        block = beams.at[lax.rem(pos + shift, many)]
        for row in range(0, height, step):
            part = len(inward)
            inward.append(pltpu.make_async_copy(block.at[pl.ds(first + row, step)], held.at[part], in_sems.at[part]))
            outward.append(pltpu.make_async_copy(held.at[part], out.at[pl.ds(row, step)], out_sems.at[part]))
    for copy in inward:
        copy.start()
    for there, back in zip(inward, outward):
        there.wait()
        back.start()
    for copy in outward:
        copy.wait()


def cut_kernel_near(cuts, step, beams, *refs):
    outs, sems = refs[: len(cuts)], refs[len(cuts)]
    pos, many = lax.axis_index("ma"), lax.axis_size("ma")
    copies = []
    for (shift, first, height), out in zip(cuts, outs):
        block = beams.at[lax.rem(pos + shift, many)]
        for row in range(0, height, step):
            source, sem = block.at[pl.ds(first + row, step)], sems.at[len(copies)]
            copies.append(pltpu.make_async_copy(source, out.at[pl.ds(row, step)], sem))
    for copy in copies:
        copy.start()
    for copy in copies:
        copy.wait()


def cut_near(beams, *cuts):
    step = 64
    parts = sum(height for _, _, height in cuts) // step
    return pl.pallas_call(
        functools.partial(cut_kernel_near, cuts, step),
        out_shape=[pltpu.VMEM((height, beams.shape[2]), beams.dtype) for _, _, height in cuts],
        in_specs=[pl.BlockSpec(memory_space=pl.ANY)],
        out_specs=[pl.BlockSpec(memory_space=pltpu.VMEM)] * len(cuts),
        scratch_shapes=[pltpu.SemaphoreType.DMA((parts,))],
        compiler_params=pltpu.CompilerParams(vmem_limit_bytes=VMEM),
        cost_estimate=pl.CostEstimate(flops=10**12, bytes_accessed=1, transcendentals=0),
        name="near",
    )(beams)


def cut_out(beams, *cuts):
    step = 32
    parts = sum(height for _, _, height in cuts) // step
    whole = pl.BlockSpec(memory_space=pl.ANY)
    return pl.pallas_call(
        functools.partial(cut_kernel, cuts, step),
        out_shape=[jax.ShapeDtypeStruct((height, beams.shape[2]), beams.dtype) for _, _, height in cuts],
        in_specs=[whole],
        out_specs=[whole] * len(cuts),
        scratch_shapes=[
            pltpu.VMEM((parts, step, beams.shape[2]), beams.dtype),
            pltpu.SemaphoreType.DMA((parts,)),
            pltpu.SemaphoreType.DMA((parts,)),
        ],
        compiler_params=pltpu.CompilerParams(vmem_limit_bytes=VMEM),
        cost_estimate=pl.CostEstimate(flops=10**12, bytes_accessed=1, transcendentals=0),
        name="cut",
    )(beams)


def along(array, by):
    count = lax.axis_size("ma")
    return lax.ppermute(array, "ma", [(i, (i + by) % count) for i in range(count)])


def beside(array, source, per_band):
    many, groups = lax.axis_size("ma"), lax.axis_size("af")
    pairs = []
    for pos in range(many):
        for group in range(groups):
            channel = (pos + source) % many
            target = group + 1 if channel >= many // 2 else group - 1
            if 0 <= target < groups and target // per_band == group // per_band:
                pairs.append((pos * groups + group, pos * groups + target))
    return lax.ppermute(array, ("ma", "af"), pairs)


def body(beams, spectrum, partners):
    many, _, _, rows, width = beams.shape
    per_band = BAND // many
    beams = beams.reshape(many, rows, width)

    downward, upward = cut_near(beams, (3, 0, rows), (1, 0, rows))
    plan = make_plan(partners, CAPS)
    again, plan = ORDER((beams, plan))
    own, far0, far1 = cut_out(again, (0, 0, rows), (2, 0, FIRST_ROWS), (2, FIRST_ROWS, rows - FIRST_ROWS))

    near1 = along(downward, -1)
    near3 = along(upward, 1)
    side0 = beside(own, 0, per_band)
    far0, near1 = ORDER((far0, near1))
    late0 = along(far0, 2)
    far1, near1, near3 = ORDER((far1, near1, near3))
    late1 = along(far1, 2)
    side1 = beside(near1, 1, per_band)
    side3 = beside(near3, 3, per_band)

    ready, fill = (), (0, 1, 2, 3, 6, 7, 8, 9)
    pieces = {(0, 0): beams, (1, 0): near1, (3, 0): near3, (4, 0): side0}
    out, held = run_stage("early", (2,), plan[0], spectrum, pieces, ready, fill, None, None, WEIGHTS[0])

    late0, out = ORDER((late0, out))
    side_first = beside(late0, 2, per_band)
    ready, fill = ready + fill, (4, 10, 11, 14, 15)
    pieces = {(2, 0): late0, (5, 0): side1, (7, 0): side3}
    out, held = run_stage("middle", (0, 1, 2), plan[1], spectrum, pieces, ready, fill, held, out, WEIGHTS[1])

    late1, out = ORDER((late1, out))
    side_second = beside(late1, 2, per_band)
    side_first, out = ORDER((side_first, out))
    ready, fill = ready + fill, (5, 12)
    pieces = {(2, 0): late0, (2, FIRST_ROWS): late1, (6, 0): side_first}
    out, held = run_stage("late", (0, 1, 2), plan[2], spectrum, pieces, ready, fill, held, out, WEIGHTS[2])

    side_second, out = ORDER((side_second, out))
    ready, fill = ready + fill, (13,)
    pieces = {(6, 0): side_first, (6, FIRST_ROWS): side_second}
    out, held = run_stage("last", (1,), plan[3], spectrum, pieces, ready, fill, held, out, WEIGHTS[3])
    return out[None]


def solution(mesh):
    in_specs = (P(None, "af", "ma", None, None), P("af", None, None), P("af", None))
    out_specs = P("ma", "af", None, None, None, None)
    return jax.shard_map(body, mesh=mesh, in_specs=in_specs, out_specs=out_specs, check_vma=False)
```

```python
import functools

import jax
import jax.numpy as jnp
from jax import lax
from jax.experimental import pallas as pl
from jax.experimental.pallas import tpu as pltpu
from jax.sharding import PartitionSpec as P

BAND = 64
HALF = 256
LATE = 2
VMEM = 56 * 2**20
STAGE_VMEM = 47 * 2**20
CAPS = (9, 10)
FIRST_ROWS = 256
NEAR = 128
WEIGHTS = (10**12, 10**12, 0, 0)
NT = (((1,), (1,)), ((), ()))
ORDER = lax.optimization_barrier


def plan_kernel(stages, caps, partners, *refs):
    lists, loads = refs[:stages], refs[stages]
    chans, slots = partners.shape
    last = 2 * chans * slots
    pos = lax.axis_index("ma")
    group = lax.axis_index("af")
    for stage in range(stages):
        lists[stage][last, 0] = 0
        loads[stage] = 0

    def put(when, stage, kind, half, channel, slot, own, source):
        @pl.when(when)
        def _():
            jobs = lists[stage - 1]
            count = jobs[last, 0]
            own_part = 1 << half if kind == 0 else 3
            source_part = 1 << half if kind == 1 else 3
            mask = jnp.left_shift(own_part, own * 2) | jnp.left_shift(source_part, source * 2)
            for place, field in enumerate((kind, half, channel, slot, own, source, mask)):
                jobs[count, place] = field
            jobs[last, 0] = count + 1
            loads[stage - 1] = loads[stage - 1] + (2 if kind == 2 else 1)

    def visit(late):
        def one(index, carry):
            channel = lax.div(index, slots)
            slot = lax.rem(index, slots)
            offset = partners[channel, slot] - group * chans
            own = lax.rem(channel - pos + 4, 4)
            partner = lax.rem(offset - pos + 8, 4)
            outside = jnp.logical_or(offset < 0, offset >= chans)
            inside = jnp.logical_not(outside)
            source = jnp.where(outside, partner + 4, partner)
            own_late, own_early = own == LATE, own != LATE
            other_late, other_early = partner == LATE, partner != LATE
            early = jnp.logical_or(inside, partner == 0)
            plain = own_early & other_early
            names = dict(channel=channel, slot=slot, own=own, source=source)
            if late:
                put(own_late & other_early, 2, 0, 0, **names)
                put(own_early & other_late & inside, 2, 1, 0, **names)
                put(own_late & other_early, 3, 0, 1, **names)
                put(own_late & other_late & inside, 3, 2, 0, **names)
                put(own_early & other_late & inside, 3, 1, 1, **names)
                put(own_early & other_late & outside, 3, 1, 0, **names)
                put(own_early & other_late & outside, 4, 1, 1, **names)
            else:
                left = plain
                for stage, may in ((1, early), (2, True)):
                    fits = jnp.logical_and(loads[stage - 1] < caps[stage - 1], may)
                    put(left & fits, stage, 2, 0, **names)
                    left = left & jnp.logical_not(fits)
                put(left, 3, 2, 0, **names)
            return carry

        lax.fori_loop(0, chans * slots, one, 0)

    visit(True)
    visit(False)


def make_plan(partners, caps):
    chans, slots = partners.shape
    stages = 4
    scalars = pl.BlockSpec(memory_space=pltpu.SMEM)
    return pl.pallas_call(
        functools.partial(plan_kernel, stages, caps),
        out_shape=[jax.ShapeDtypeStruct((2 * chans * slots + 1, 7), jnp.int32)] * stages,
        in_specs=[scalars],
        out_specs=[scalars] * stages,
        scratch_shapes=[pltpu.SMEM((stages,), jnp.int32)],
        cost_estimate=pl.CostEstimate(flops=10**12, bytes_accessed=1, transcendentals=0),
        name="plan",
    )(partners)


def kernel(kinds, names, ready, fill, keep, *refs):
    jobs, spectrum = refs[:2]
    pieces = dict(zip(names, refs[2 : 2 + len(names)]))
    out, held, state, rows_out, columns_out, whole_out, in_sems, out_sems = refs[-8:]
    outs = (rows_out, columns_out, whole_out)
    pos = lax.axis_index("ma")
    total = jobs[jobs.shape[0] - 1, 0]

    places = {}
    for (source, first), ref in pieces.items():
        if source == 0:
            ref = ref.at[pos]
        for half in range(2):
            low, high = max(first, half * HALF), min(first + ref.shape[0], half * HALF + HALF)
            if low < high and source * 2 + half in fill:
                into = held.at[source * 2 + half, pl.ds(low - half * HALF, high - low)]
                places.setdefault(source * 2 + half, []).append((ref.at[pl.ds(low - first, high - low)], into))
    fresh = sum(1 << part for part in places)
    state[0] = ready
    state[1] = ready

    def each(mask, act):
        @pl.when(mask != 0)
        def _():
            for part, copies in places.items():

                @pl.when(jnp.bitwise_and(mask, 1 << part) != 0)
                def _():
                    for copy in copies:
                        act(pltpu.make_async_copy(*copy, in_sems.at[part]))

    def fetch(wanted):
        mask = wanted & ~state[0]
        each(mask, lambda copy: copy.start())
        state[0] = state[0] | mask

    def arrive(wanted):
        mask = wanted & ~state[1]
        each(mask, lambda copy: copy.wait())
        state[1] = state[1] | mask

    def scaled(block, weights):
        block = block.astype(jnp.float32)
        width = weights.shape[-1]
        real = (block[:, :width] * weights).astype(jnp.bfloat16)
        imag = (block[:, width:] * weights).astype(jnp.bfloat16)
        upper = jnp.concatenate([real, imag], axis=1)
        lower = jnp.concatenate([imag, -real], axis=1)
        return jnp.concatenate([upper, lower], axis=0)

    def write(kind, job, place):
        target = out.at[jobs[job, 2], jobs[job, 3]]
        some = pl.ds(pl.multiple_of(jobs[job, 1] * HALF, HALF), HALF)
        if kind == 0:
            target = target.at[:, some, :]
        if kind == 1:
            target = target.at[:, :, some]
        return pltpu.make_async_copy(outs[kind].at[place], target, out_sems.at[place])

    def drain(job):
        for kind in kinds:

            @pl.when(jobs[job, 0] == kind)
            def _():
                write(kind, job, lax.rem(job, 2)).wait()

    @pl.when(total > 0)
    def _():
        fetch(jobs[0, 6])

    if keep:
        fetch(jnp.int32(fresh))

    def step(job, carry):
        place = lax.rem(job, 2)
        half, own, partner = jobs[job, 1], jobs[job, 4], jobs[job, 5]
        arrive(jobs[job, 6])
        if not keep:

            @pl.when(job + 1 < total)
            def _():
                fetch(jobs[job + 1, 6])

        @pl.when(job >= 2)
        def _():
            drain(job - 2)

        weights = spectrum[jobs[job, 2], pl.ds(jobs[job, 3], 1), :]

        def taken(source, whole):
            if not whole:
                return held[source * 2 + half]
            block = held[pl.ds(source * 2, 2)]
            return block.reshape(2 * HALF, block.shape[2])

        for kind in kinds:

            @pl.when(jobs[job, 0] == kind)
            def _():
                left = scaled(taken(own, kind != 0), weights)
                right = taken(partner, kind != 1)
                product = lax.dot_general(left, right, NT, preferred_element_type=jnp.float32)
                outs[kind][place] = product.astype(jnp.bfloat16).reshape(outs[kind].shape[1:])
                write(kind, job, place).start()

        return carry

    lax.fori_loop(0, total, step, 0)
    if keep:
        arrive(jnp.int32(fresh))

    @pl.when(total >= 2)
    def _():
        drain(total - 2)

    @pl.when(total >= 1)
    def _():
        drain(total - 1)


def run_stage(name, kinds, jobs, spectrum, pieces, ready, fill, held, out, weight):
    chans, slots, _ = spectrum.shape
    names = tuple(pieces)
    arrays = [pieces[name] for name in names]
    rows, width = 2 * HALF, arrays[0].shape[-1]
    whole = pl.BlockSpec(memory_space=pl.ANY)
    vector = pl.BlockSpec(memory_space=pltpu.VMEM)
    operands = [jobs, spectrum, *arrays]
    specs = [pl.BlockSpec(memory_space=pltpu.SMEM), vector] + [whole] * len(arrays)
    aliases = {}
    if out is not None:
        aliases = {len(operands): 0, len(operands) + 1: 1}
        operands += [out, held]
        specs += [whole, vector]
    return pl.pallas_call(
        functools.partial(kernel, kinds, names, sum(1 << part for part in ready), fill, name != "last"),
        out_shape=[
            jax.ShapeDtypeStruct((chans, slots, 2, rows, rows), jnp.bfloat16),
            pltpu.VMEM((16, HALF, width), jnp.bfloat16),
        ],
        in_specs=specs,
        out_specs=[whole, vector],
        input_output_aliases=aliases,
        scratch_shapes=[
            pltpu.SMEM((2,), jnp.int32),
            pltpu.VMEM((2, 2, HALF, rows), jnp.bfloat16),
            pltpu.VMEM((2, 2, rows, HALF), jnp.bfloat16),
            pltpu.VMEM((2, 2, rows, rows), jnp.bfloat16),
            pltpu.SemaphoreType.DMA((16,)),
            pltpu.SemaphoreType.DMA((2,)),
        ],
        compiler_params=pltpu.CompilerParams(vmem_limit_bytes=STAGE_VMEM),
        cost_estimate=pl.CostEstimate(flops=weight, bytes_accessed=weight, transcendentals=0),
        name=name,
    )(*operands)


def cut_kernel(cuts, step, beams, *refs):
    outs, (held, in_sems, out_sems) = refs[: len(cuts)], refs[len(cuts) :]
    pos, many = lax.axis_index("ma"), lax.axis_size("ma")
    inward, outward = [], []
    for (shift, first, height), out in zip(cuts, outs):
        block = beams.at[lax.rem(pos + shift, many)]
        for row in range(0, height, step):
            part = len(inward)
            inward.append(pltpu.make_async_copy(block.at[pl.ds(first + row, step)], held.at[part], in_sems.at[part]))
            outward.append(pltpu.make_async_copy(held.at[part], out.at[pl.ds(row, step)], out_sems.at[part]))
    for copy in inward:
        copy.start()
    for there, back in zip(inward, outward):
        there.wait()
        back.start()
    for copy in outward:
        copy.wait()


def cut_kernel_near(cuts, step, beams, *refs):
    outs, sems = refs[: len(cuts)], refs[len(cuts)]
    pos, many = lax.axis_index("ma"), lax.axis_size("ma")
    copies = []
    for (shift, first, height), out in zip(cuts, outs):
        block = beams.at[lax.rem(pos + shift, many)]
        for row in range(0, height, step):
            source, sem = block.at[pl.ds(first + row, step)], sems.at[len(copies)]
            copies.append(pltpu.make_async_copy(source, out.at[pl.ds(row, step)], sem))
    for copy in copies:
        copy.start()
    for copy in copies:
        copy.wait()


def cut_near(beams, *cuts):
    step = 64
    parts = sum(height for _, _, height in cuts) // step
    return pl.pallas_call(
        functools.partial(cut_kernel_near, cuts, step),
        out_shape=[pltpu.VMEM((height, beams.shape[2]), beams.dtype) for _, _, height in cuts],
        in_specs=[pl.BlockSpec(memory_space=pl.ANY)],
        out_specs=[pl.BlockSpec(memory_space=pltpu.VMEM)] * len(cuts),
        scratch_shapes=[pltpu.SemaphoreType.DMA((parts,))],
        compiler_params=pltpu.CompilerParams(vmem_limit_bytes=VMEM),
        cost_estimate=pl.CostEstimate(flops=10**12, bytes_accessed=1, transcendentals=0),
        name="near",
    )(beams)


def cut_out(beams, *cuts):
    step = 32
    parts = sum(height for _, _, height in cuts) // step
    whole = pl.BlockSpec(memory_space=pl.ANY)
    return pl.pallas_call(
        functools.partial(cut_kernel, cuts, step),
        out_shape=[jax.ShapeDtypeStruct((height, beams.shape[2]), beams.dtype) for _, _, height in cuts],
        in_specs=[whole],
        out_specs=[whole] * len(cuts),
        scratch_shapes=[
            pltpu.VMEM((parts, step, beams.shape[2]), beams.dtype),
            pltpu.SemaphoreType.DMA((parts,)),
            pltpu.SemaphoreType.DMA((parts,)),
        ],
        compiler_params=pltpu.CompilerParams(vmem_limit_bytes=VMEM),
        cost_estimate=pl.CostEstimate(flops=10**12, bytes_accessed=1, transcendentals=0),
        name="cut",
    )(beams)


def along(array, by):
    count = lax.axis_size("ma")
    return lax.ppermute(array, "ma", [(i, (i + by) % count) for i in range(count)])


def beside(array, source, per_band):
    many, groups = lax.axis_size("ma"), lax.axis_size("af")
    pairs = []
    for pos in range(many):
        for group in range(groups):
            channel = (pos + source) % many
            target = group + 1 if channel >= many // 2 else group - 1
            if 0 <= target < groups and target // per_band == group // per_band:
                pairs.append((pos * groups + group, pos * groups + target))
    return lax.ppermute(array, ("ma", "af"), pairs)


def body(beams, spectrum, partners):
    many, _, _, rows, width = beams.shape
    per_band = BAND // many
    beams = beams.reshape(many, rows, width)

    down, up = [None, None], [None, None]
    down[0], up[0] = cut_near(beams, (3, 0, NEAR), (1, 0, NEAR))
    again, down[0], up[0] = ORDER((beams, down[0], up[0]))
    down[1], up[1] = cut_near(again, (3, NEAR, rows - NEAR), (1, NEAR, rows - NEAR))
    again, down[1], up[1] = ORDER((beams, down[1], up[1]))
    own, far0, far1 = cut_out(again, (0, 0, rows), (2, 0, FIRST_ROWS), (2, FIRST_ROWS, rows - FIRST_ROWS))
    plan = make_plan(partners, CAPS)

    near1 = [along(part, -1) for part in down]
    near3 = [along(part, 1) for part in up]
    side0 = beside(own, 0, per_band)
    side1 = [beside(near1[0], 1, per_band)]
    side3 = [beside(near3[0], 3, per_band)]
    far0, near1[1], side1[0], side3[0] = ORDER((far0, near1[1], side1[0], side3[0]))
    late0 = along(far0, 2)
    far1, near1[1], near3[1], side0 = ORDER((far1, near1[1], near3[1], side0))
    late1 = along(far1, 2)
    side1.append(beside(near1[1], 1, per_band))
    side3.append(beside(near3[1], 3, per_band))

    ready, fill = (), (0, 1, 2, 3, 6, 7, 8, 9)
    pieces = {(0, 0): beams, (4, 0): side0}
    pieces |= {(1, 0): near1[0], (1, NEAR): near1[1], (3, 0): near3[0], (3, NEAR): near3[1]}
    out, held = run_stage("early", (2,), plan[0], spectrum, pieces, ready, fill, None, None, WEIGHTS[0])

    late0, out = ORDER((late0, out))
    side_first = beside(late0, 2, per_band)
    ready, fill = ready + fill, (4, 10, 11, 14, 15)
    pieces = {(2, 0): late0, (5, 0): side1[0], (5, NEAR): side1[1], (7, 0): side3[0], (7, NEAR): side3[1]}
    out, held = run_stage("middle", (0, 1, 2), plan[1], spectrum, pieces, ready, fill, held, out, WEIGHTS[1])

    late1, out = ORDER((late1, out))
    side_second = beside(late1, 2, per_band)
    side_first, out = ORDER((side_first, out))
    ready, fill = ready + fill, (5, 12)
    pieces = {(2, 0): late0, (2, FIRST_ROWS): late1, (6, 0): side_first}
    out, held = run_stage("late", (0, 1, 2), plan[2], spectrum, pieces, ready, fill, held, out, WEIGHTS[2])

    side_second, out = ORDER((side_second, out))
    ready, fill = ready + fill, (13,)
    pieces = {(6, 0): side_first, (6, FIRST_ROWS): side_second}
    out, held = run_stage("last", (1,), plan[3], spectrum, pieces, ready, fill, held, out, WEIGHTS[3])
    return out[None]


def solution(mesh):
    in_specs = (P(None, "af", "ma", None, None), P("af", None, None), P("af", None))
    out_specs = P("ma", "af", None, None, None, None)
    return jax.shard_map(body, mesh=mesh, in_specs=in_specs, out_specs=out_specs, check_vma=False)
```

```python
import functools

import jax
import jax.numpy as jnp
from jax import lax
from jax.experimental import pallas as pl
from jax.experimental.pallas import tpu as pltpu
from jax.sharding import PartitionSpec as P

BAND = 64
HALF = 256
LATE = 2
VMEM = 56 * 2**20
STAGE_VMEM = 47 * 2**20
CAPS = (9, 10)
FIRST_ROWS = 256
NEAR = 128
WEIGHTS = (10**12, 10**12, 0, 0)
NT = (((1,), (1,)), ((), ()))
ORDER = lax.optimization_barrier


def plan_kernel(stages, caps, partners, *refs):
    lists, loads = refs[:stages], refs[stages]
    chans, slots = partners.shape
    last = 2 * chans * slots
    pos = lax.axis_index("ma")
    group = lax.axis_index("af")
    for stage in range(stages):
        lists[stage][last, 0] = 0
        loads[stage] = 0

    def put(when, stage, kind, half, channel, slot, own, source):
        @pl.when(when)
        def _():
            jobs = lists[stage - 1]
            count = jobs[last, 0]
            own_part = 1 << half if kind == 0 else 3
            source_part = 1 << half if kind == 1 else 3
            mask = jnp.left_shift(own_part, own * 2) | jnp.left_shift(source_part, source * 2)
            for place, field in enumerate((kind, half, channel, slot, own, source, mask)):
                jobs[count, place] = field
            jobs[last, 0] = count + 1
            loads[stage - 1] = loads[stage - 1] + (2 if kind == 2 else 1)

    def visit(late):
        def one(index, carry):
            channel = lax.div(index, slots)
            slot = lax.rem(index, slots)
            offset = partners[channel, slot] - group * chans
            own = lax.rem(channel - pos + 4, 4)
            partner = lax.rem(offset - pos + 8, 4)
            outside = jnp.logical_or(offset < 0, offset >= chans)
            inside = jnp.logical_not(outside)
            source = jnp.where(outside, partner + 4, partner)
            own_late, own_early = own == LATE, own != LATE
            other_late, other_early = partner == LATE, partner != LATE
            early = jnp.logical_or(inside, partner == 0)
            plain = own_early & other_early
            names = dict(channel=channel, slot=slot, own=own, source=source)
            if late:
                put(own_late & other_early, 2, 0, 0, **names)
                put(own_early & other_late & inside, 2, 1, 0, **names)
                put(own_late & other_early, 3, 0, 1, **names)
                put(own_late & other_late & inside, 3, 2, 0, **names)
                put(own_early & other_late & inside, 3, 1, 1, **names)
                put(own_early & other_late & outside, 3, 1, 0, **names)
                put(own_early & other_late & outside, 4, 1, 1, **names)
            else:
                left = plain
                for stage, may in ((1, early), (2, True)):
                    fits = jnp.logical_and(loads[stage - 1] < caps[stage - 1], may)
                    put(left & fits, stage, 2, 0, **names)
                    left = left & jnp.logical_not(fits)
                put(left, 3, 2, 0, **names)
            return carry

        lax.fori_loop(0, chans * slots, one, 0)

    visit(True)
    visit(False)


def make_plan(partners, caps):
    chans, slots = partners.shape
    stages = 4
    scalars = pl.BlockSpec(memory_space=pltpu.SMEM)
    return pl.pallas_call(
        functools.partial(plan_kernel, stages, caps),
        out_shape=[jax.ShapeDtypeStruct((2 * chans * slots + 1, 7), jnp.int32)] * stages,
        in_specs=[scalars],
        out_specs=[scalars] * stages,
        scratch_shapes=[pltpu.SMEM((stages,), jnp.int32)],
        cost_estimate=pl.CostEstimate(flops=10**12, bytes_accessed=1, transcendentals=0),
        name="plan",
    )(partners)


def kernel(kinds, names, ready, fill, keep, *refs):
    jobs, spectrum = refs[:2]
    pieces = dict(zip(names, refs[2 : 2 + len(names)]))
    out, held, state, rows_out, columns_out, whole_out, in_sems, out_sems = refs[-8:]
    outs = (rows_out, columns_out, whole_out)
    pos = lax.axis_index("ma")
    total = jobs[jobs.shape[0] - 1, 0]

    places = {}
    for (source, first), ref in pieces.items():
        if source == 0:
            ref = ref.at[pos]
        for half in range(2):
            low, high = max(first, half * HALF), min(first + ref.shape[0], half * HALF + HALF)
            if low < high and source * 2 + half in fill:
                into = held.at[source * 2 + half, pl.ds(low - half * HALF, high - low)]
                places.setdefault(source * 2 + half, []).append((ref.at[pl.ds(low - first, high - low)], into))
    fresh = sum(1 << part for part in places)
    state[0] = ready
    state[1] = ready

    def each(mask, act):
        @pl.when(mask != 0)
        def _():
            for part, copies in places.items():

                @pl.when(jnp.bitwise_and(mask, 1 << part) != 0)
                def _():
                    for copy in copies:
                        act(pltpu.make_async_copy(*copy, in_sems.at[part]))

    def fetch(wanted):
        mask = wanted & ~state[0]
        each(mask, lambda copy: copy.start())
        state[0] = state[0] | mask

    def arrive(wanted):
        mask = wanted & ~state[1]
        each(mask, lambda copy: copy.wait())
        state[1] = state[1] | mask

    def scaled(block, weights):
        block = block.astype(jnp.float32)
        width = weights.shape[-1]
        real = (block[:, :width] * weights).astype(jnp.bfloat16)
        imag = (block[:, width:] * weights).astype(jnp.bfloat16)
        upper = jnp.concatenate([real, imag], axis=1)
        lower = jnp.concatenate([imag, -real], axis=1)
        return jnp.concatenate([upper, lower], axis=0)

    def write(kind, job, place):
        target = out.at[jobs[job, 2], jobs[job, 3]]
        some = pl.ds(pl.multiple_of(jobs[job, 1] * HALF, HALF), HALF)
        if kind == 0:
            target = target.at[:, some, :]
        if kind == 1:
            target = target.at[:, :, some]
        return pltpu.make_async_copy(outs[kind].at[place], target, out_sems.at[place])

    def drain(job):
        for kind in kinds:

            @pl.when(jobs[job, 0] == kind)
            def _():
                write(kind, job, lax.rem(job, 2)).wait()

    @pl.when(total > 0)
    def _():
        fetch(jobs[0, 6])

    if keep:
        fetch(jnp.int32(fresh))

    def step(job, carry):
        place = lax.rem(job, 2)
        half, own, partner = jobs[job, 1], jobs[job, 4], jobs[job, 5]
        arrive(jobs[job, 6])
        if not keep:

            @pl.when(job + 1 < total)
            def _():
                fetch(jobs[job + 1, 6])

        @pl.when(job >= 2)
        def _():
            drain(job - 2)

        weights = spectrum[jobs[job, 2], pl.ds(jobs[job, 3], 1), :]

        def taken(source, whole):
            if not whole:
                return held[source * 2 + half]
            block = held[pl.ds(source * 2, 2)]
            return block.reshape(2 * HALF, block.shape[2])

        for kind in kinds:

            @pl.when(jobs[job, 0] == kind)
            def _():
                left = scaled(taken(own, kind != 0), weights)
                right = taken(partner, kind != 1)
                product = lax.dot_general(left, right, NT, preferred_element_type=jnp.float32)
                outs[kind][place] = product.astype(jnp.bfloat16).reshape(outs[kind].shape[1:])
                write(kind, job, place).start()

        return carry

    lax.fori_loop(0, total, step, 0)
    if keep:
        arrive(jnp.int32(fresh))

    @pl.when(total >= 2)
    def _():
        drain(total - 2)

    @pl.when(total >= 1)
    def _():
        drain(total - 1)


def run_stage(name, kinds, jobs, spectrum, pieces, ready, fill, held, out, weight):
    chans, slots, _ = spectrum.shape
    names = tuple(pieces)
    arrays = [pieces[name] for name in names]
    rows, width = 2 * HALF, arrays[0].shape[-1]
    whole = pl.BlockSpec(memory_space=pl.ANY)
    vector = pl.BlockSpec(memory_space=pltpu.VMEM)
    operands = [jobs, spectrum, *arrays]
    specs = [pl.BlockSpec(memory_space=pltpu.SMEM), vector] + [whole] * len(arrays)
    aliases = {}
    if out is not None:
        aliases = {len(operands): 0, len(operands) + 1: 1}
        operands += [out, held]
        specs += [whole, vector]
    return pl.pallas_call(
        functools.partial(kernel, kinds, names, sum(1 << part for part in ready), fill, name != "last"),
        out_shape=[
            jax.ShapeDtypeStruct((chans, slots, 2, rows, rows), jnp.bfloat16),
            pltpu.VMEM((16, HALF, width), jnp.bfloat16),
        ],
        in_specs=specs,
        out_specs=[whole, vector],
        input_output_aliases=aliases,
        scratch_shapes=[
            pltpu.SMEM((2,), jnp.int32),
            pltpu.VMEM((2, 2, HALF, rows), jnp.bfloat16),
            pltpu.VMEM((2, 2, rows, HALF), jnp.bfloat16),
            pltpu.VMEM((2, 2, rows, rows), jnp.bfloat16),
            pltpu.SemaphoreType.DMA((16,)),
            pltpu.SemaphoreType.DMA((2,)),
        ],
        compiler_params=pltpu.CompilerParams(vmem_limit_bytes=STAGE_VMEM),
        cost_estimate=pl.CostEstimate(flops=weight, bytes_accessed=weight, transcendentals=0),
        name=name,
    )(*operands)


def cut_kernel(cuts, step, beams, *refs):
    outs, (held, in_sems, out_sems) = refs[: len(cuts)], refs[len(cuts) :]
    pos, many = lax.axis_index("ma"), lax.axis_size("ma")
    inward, outward = [], []
    for (shift, first, height), out in zip(cuts, outs):
        block = beams.at[lax.rem(pos + shift, many)]
        for row in range(0, height, step):
            part = len(inward)
            inward.append(pltpu.make_async_copy(block.at[pl.ds(first + row, step)], held.at[part], in_sems.at[part]))
            outward.append(pltpu.make_async_copy(held.at[part], out.at[pl.ds(row, step)], out_sems.at[part]))
    for copy in inward:
        copy.start()
    for there, back in zip(inward, outward):
        there.wait()
        back.start()
    for copy in outward:
        copy.wait()


def cut_kernel_near(cuts, step, beams, *refs):
    outs, sems = refs[: len(cuts)], refs[len(cuts)]
    pos, many = lax.axis_index("ma"), lax.axis_size("ma")
    copies = []
    for (shift, first, height), out in zip(cuts, outs):
        block = beams.at[lax.rem(pos + shift, many)]
        for row in range(0, height, step):
            source, sem = block.at[pl.ds(first + row, step)], sems.at[len(copies)]
            copies.append(pltpu.make_async_copy(source, out.at[pl.ds(row, step)], sem))
    for copy in copies:
        copy.start()
    for copy in copies:
        copy.wait()


def cut_near(beams, *cuts):
    step = 64
    parts = sum(height for _, _, height in cuts) // step
    return pl.pallas_call(
        functools.partial(cut_kernel_near, cuts, step),
        out_shape=[pltpu.VMEM((height, beams.shape[2]), beams.dtype) for _, _, height in cuts],
        in_specs=[pl.BlockSpec(memory_space=pl.ANY)],
        out_specs=[pl.BlockSpec(memory_space=pltpu.VMEM)] * len(cuts),
        scratch_shapes=[pltpu.SemaphoreType.DMA((parts,))],
        compiler_params=pltpu.CompilerParams(vmem_limit_bytes=VMEM),
        cost_estimate=pl.CostEstimate(flops=10**12, bytes_accessed=1, transcendentals=0),
        name="near",
    )(beams)


def cut_out(beams, *cuts):
    step = 32
    parts = sum(height for _, _, height in cuts) // step
    whole = pl.BlockSpec(memory_space=pl.ANY)
    return pl.pallas_call(
        functools.partial(cut_kernel, cuts, step),
        out_shape=[jax.ShapeDtypeStruct((height, beams.shape[2]), beams.dtype) for _, _, height in cuts],
        in_specs=[whole],
        out_specs=[whole] * len(cuts),
        scratch_shapes=[
            pltpu.VMEM((parts, step, beams.shape[2]), beams.dtype),
            pltpu.SemaphoreType.DMA((parts,)),
            pltpu.SemaphoreType.DMA((parts,)),
        ],
        compiler_params=pltpu.CompilerParams(vmem_limit_bytes=VMEM),
        cost_estimate=pl.CostEstimate(flops=10**12, bytes_accessed=1, transcendentals=0),
        name="cut",
    )(beams)


def along(array, by):
    count = lax.axis_size("ma")
    return lax.ppermute(array, "ma", [(i, (i + by) % count) for i in range(count)])


def beside(array, source, per_band):
    many, groups = lax.axis_size("ma"), lax.axis_size("af")
    pairs = []
    for pos in range(many):
        for group in range(groups):
            channel = (pos + source) % many
            target = group + 1 if channel >= many // 2 else group - 1
            if 0 <= target < groups and target // per_band == group // per_band:
                pairs.append((pos * groups + group, pos * groups + target))
    return lax.ppermute(array, ("ma", "af"), pairs)


def body(beams, spectrum, partners):
    many, _, _, rows, width = beams.shape
    per_band = BAND // many
    beams = beams.reshape(many, rows, width)

    down, up = [None, None], [None, None]
    pos = lax.axis_index("ma")
    down[0], up[0] = (
        lax.dynamic_slice(beams, (lax.rem(pos + shift, many), 0, 0), (1, NEAR, width))[0] for shift in (3, 1)
    )
    again, down[0], up[0] = ORDER((beams, down[0], up[0]))
    down[1], up[1] = cut_near(again, (3, NEAR, rows - NEAR), (1, NEAR, rows - NEAR))
    again, down[1], up[1] = ORDER((beams, down[1], up[1]))
    own, far0, far1 = cut_out(again, (0, 0, rows), (2, 0, FIRST_ROWS), (2, FIRST_ROWS, rows - FIRST_ROWS))
    plan = make_plan(partners, CAPS)

    near1 = [along(part, -1) for part in down]
    near3 = [along(part, 1) for part in up]
    side0 = beside(own, 0, per_band)
    side1 = [beside(near1[0], 1, per_band)]
    side3 = [beside(near3[0], 3, per_band)]
    far0, near1[1], side1[0], side3[0] = ORDER((far0, near1[1], side1[0], side3[0]))
    late0 = along(far0, 2)
    far1, near1[1], near3[1], side0 = ORDER((far1, near1[1], near3[1], side0))
    late1 = along(far1, 2)
    side1.append(beside(near1[1], 1, per_band))
    side3.append(beside(near3[1], 3, per_band))

    ready, fill = (), (0, 1, 2, 3, 6, 7, 8, 9)
    pieces = {(0, 0): beams, (4, 0): side0}
    pieces |= {(1, 0): near1[0], (1, NEAR): near1[1], (3, 0): near3[0], (3, NEAR): near3[1]}
    out, held = run_stage("early", (2,), plan[0], spectrum, pieces, ready, fill, None, None, WEIGHTS[0])

    late0, out = ORDER((late0, out))
    side_first = beside(late0, 2, per_band)
    ready, fill = ready + fill, (4, 10, 11, 14, 15)
    pieces = {(2, 0): late0, (5, 0): side1[0], (5, NEAR): side1[1], (7, 0): side3[0], (7, NEAR): side3[1]}
    out, held = run_stage("middle", (0, 1, 2), plan[1], spectrum, pieces, ready, fill, held, out, WEIGHTS[1])

    late1, out = ORDER((late1, out))
    side_second = beside(late1, 2, per_band)
    side_first, out = ORDER((side_first, out))
    ready, fill = ready + fill, (5, 12)
    pieces = {(2, 0): late0, (2, FIRST_ROWS): late1, (6, 0): side_first}
    out, held = run_stage("late", (0, 1, 2), plan[2], spectrum, pieces, ready, fill, held, out, WEIGHTS[2])

    side_second, out = ORDER((side_second, out))
    ready, fill = ready + fill, (13,)
    pieces = {(6, 0): side_first, (6, FIRST_ROWS): side_second}
    out, held = run_stage("last", (1,), plan[3], spectrum, pieces, ready, fill, held, out, WEIGHTS[3])
    return out[None]


def solution(mesh):
    in_specs = (P(None, "af", "ma", None, None), P("af", None, None), P("af", None))
    out_specs = P("ma", "af", None, None, None, None)
    return jax.shard_map(body, mesh=mesh, in_specs=in_specs, out_specs=out_specs, check_vma=False)
```

```python
import functools

import jax
import jax.numpy as jnp
from jax import lax
from jax.experimental import pallas as pl
from jax.experimental.pallas import tpu as pltpu
from jax.sharding import PartitionSpec as P

BAND = 64
HALF = 256
LATE = 2
VMEM = 56 * 2**20
STAGE_VMEM = 47 * 2**20
CAPS = (9, 10)
FIRST_ROWS = 256
NEAR = 128
WEIGHTS = (10**12, 10**12, 0, 0)
NT = (((1,), (1,)), ((), ()))
ORDER = lax.optimization_barrier


def plan_kernel(stages, caps, partners, *refs):
    lists, loads = refs[:stages], refs[stages]
    chans, slots = partners.shape
    last = 2 * chans * slots
    pos = lax.axis_index("ma")
    group = lax.axis_index("af")
    for stage in range(stages):
        lists[stage][last, 0] = 0
        loads[stage] = 0

    def put(when, stage, kind, half, channel, slot, own, source):
        @pl.when(when)
        def _():
            jobs = lists[stage - 1]
            count = jobs[last, 0]
            own_part = 1 << half if kind == 0 else 3
            source_part = 1 << half if kind == 1 else 3
            mask = jnp.left_shift(own_part, own * 2) | jnp.left_shift(source_part, source * 2)
            for place, field in enumerate((kind, half, channel, slot, own, source, mask)):
                jobs[count, place] = field
            jobs[last, 0] = count + 1
            loads[stage - 1] = loads[stage - 1] + (2 if kind == 2 else 1)

    def visit(late):
        def one(index, carry):
            channel = lax.div(index, slots)
            slot = lax.rem(index, slots)
            offset = partners[channel, slot] - group * chans
            own = lax.rem(channel - pos + 4, 4)
            partner = lax.rem(offset - pos + 8, 4)
            outside = jnp.logical_or(offset < 0, offset >= chans)
            inside = jnp.logical_not(outside)
            source = jnp.where(outside, partner + 4, partner)
            own_late, own_early = own == LATE, own != LATE
            other_late, other_early = partner == LATE, partner != LATE
            early = jnp.logical_or(inside, partner == 0)
            plain = own_early & other_early
            names = dict(channel=channel, slot=slot, own=own, source=source)
            if late:
                put(own_late & other_early, 2, 0, 0, **names)
                put(own_early & other_late & inside, 2, 1, 0, **names)
                put(own_late & other_early, 3, 0, 1, **names)
                put(own_late & other_late & inside, 3, 2, 0, **names)
                put(own_early & other_late & inside, 3, 1, 1, **names)
                put(own_early & other_late & outside, 3, 1, 0, **names)
                put(own_early & other_late & outside, 4, 1, 1, **names)
            else:
                left = plain
                for stage, may in ((1, early), (2, True)):
                    fits = jnp.logical_and(loads[stage - 1] < caps[stage - 1], may)
                    put(left & fits, stage, 2, 0, **names)
                    left = left & jnp.logical_not(fits)
                put(left, 3, 2, 0, **names)
            return carry

        lax.fori_loop(0, chans * slots, one, 0)

    visit(True)
    visit(False)


def make_plan(partners, caps):
    chans, slots = partners.shape
    stages = 4
    scalars = pl.BlockSpec(memory_space=pltpu.SMEM)
    return pl.pallas_call(
        functools.partial(plan_kernel, stages, caps),
        out_shape=[jax.ShapeDtypeStruct((2 * chans * slots + 1, 7), jnp.int32)] * stages,
        in_specs=[scalars],
        out_specs=[scalars] * stages,
        scratch_shapes=[pltpu.SMEM((stages,), jnp.int32)],
        cost_estimate=pl.CostEstimate(flops=10**12, bytes_accessed=1, transcendentals=0),
        name="plan",
    )(partners)


def kernel(kinds, names, ready, fill, keep, *refs):
    jobs, spectrum = refs[:2]
    pieces = dict(zip(names, refs[2 : 2 + len(names)]))
    out, held, state, rows_out, columns_out, whole_out, in_sems, out_sems = refs[-8:]
    outs = (rows_out, columns_out, whole_out)
    pos = lax.axis_index("ma")
    total = jobs[jobs.shape[0] - 1, 0]

    places = {}
    for (source, first), ref in pieces.items():
        if source == 0:
            ref = ref.at[pos]
        for half in range(2):
            low, high = max(first, half * HALF), min(first + ref.shape[0], half * HALF + HALF)
            if low < high and source * 2 + half in fill:
                for row in range(low, high, 64):
                    into = held.at[source * 2 + half, pl.ds(row - half * HALF, 64)]
                    places.setdefault(source * 2 + half, []).append((ref.at[pl.ds(row - first, 64)], into))
    fresh = sum(1 << part for part in places)
    state[0] = ready
    state[1] = ready

    def each(mask, act):
        @pl.when(mask != 0)
        def _():
            for part, copies in places.items():

                @pl.when(jnp.bitwise_and(mask, 1 << part) != 0)
                def _():
                    for copy in copies:
                        act(pltpu.make_async_copy(*copy, in_sems.at[part]))

    def fetch(wanted):
        mask = wanted & ~state[0]
        each(mask, lambda copy: copy.start())
        state[0] = state[0] | mask

    def arrive(wanted):
        mask = wanted & ~state[1]
        each(mask, lambda copy: copy.wait())
        state[1] = state[1] | mask

    def scaled(block, weights):
        block = block.astype(jnp.float32)
        width = weights.shape[-1]
        real = (block[:, :width] * weights).astype(jnp.bfloat16)
        imag = (block[:, width:] * weights).astype(jnp.bfloat16)
        upper = jnp.concatenate([real, imag], axis=1)
        lower = jnp.concatenate([imag, -real], axis=1)
        return jnp.concatenate([upper, lower], axis=0)

    def write(kind, job, place):
        target = out.at[jobs[job, 2], jobs[job, 3]]
        some = pl.ds(pl.multiple_of(jobs[job, 1] * HALF, HALF), HALF)
        if kind == 0:
            target = target.at[:, some, :]
        if kind == 1:
            target = target.at[:, :, some]
        return pltpu.make_async_copy(outs[kind].at[place], target, out_sems.at[place])

    def drain(job):
        for kind in kinds:

            @pl.when(jobs[job, 0] == kind)
            def _():
                write(kind, job, lax.rem(job, 2)).wait()

    @pl.when(total > 0)
    def _():
        fetch(jobs[0, 6])

    if keep:
        fetch(jnp.int32(fresh))

    def step(job, carry):
        place = lax.rem(job, 2)
        half, own, partner = jobs[job, 1], jobs[job, 4], jobs[job, 5]
        arrive(jobs[job, 6])
        if not keep:

            @pl.when(job + 1 < total)
            def _():
                fetch(jobs[job + 1, 6])

        @pl.when(job >= 2)
        def _():
            drain(job - 2)

        weights = spectrum[jobs[job, 2], pl.ds(jobs[job, 3], 1), :]

        def taken(source, whole):
            if not whole:
                return held[source * 2 + half]
            block = held[pl.ds(source * 2, 2)]
            return block.reshape(2 * HALF, block.shape[2])

        for kind in kinds:

            @pl.when(jobs[job, 0] == kind)
            def _():
                left = scaled(taken(own, kind != 0), weights)
                right = taken(partner, kind != 1)
                product = lax.dot_general(left, right, NT, preferred_element_type=jnp.float32)
                outs[kind][place] = product.astype(jnp.bfloat16).reshape(outs[kind].shape[1:])
                write(kind, job, place).start()

        return carry

    lax.fori_loop(0, total, step, 0)
    if keep:
        arrive(jnp.int32(fresh))

    @pl.when(total >= 2)
    def _():
        drain(total - 2)

    @pl.when(total >= 1)
    def _():
        drain(total - 1)


def run_stage(name, kinds, jobs, spectrum, pieces, ready, fill, held, out, weight):
    chans, slots, _ = spectrum.shape
    names = tuple(pieces)
    arrays = [pieces[name] for name in names]
    rows, width = 2 * HALF, arrays[0].shape[-1]
    whole = pl.BlockSpec(memory_space=pl.ANY)
    vector = pl.BlockSpec(memory_space=pltpu.VMEM)
    operands = [jobs, spectrum, *arrays]
    specs = [pl.BlockSpec(memory_space=pltpu.SMEM), vector] + [whole] * len(arrays)
    aliases = {}
    if out is not None:
        aliases = {len(operands): 0, len(operands) + 1: 1}
        operands += [out, held]
        specs += [whole, vector]
    return pl.pallas_call(
        functools.partial(kernel, kinds, names, sum(1 << part for part in ready), fill, name != "last"),
        out_shape=[
            jax.ShapeDtypeStruct((chans, slots, 2, rows, rows), jnp.bfloat16),
            pltpu.VMEM((16, HALF, width), jnp.bfloat16),
        ],
        in_specs=specs,
        out_specs=[whole, vector],
        input_output_aliases=aliases,
        scratch_shapes=[
            pltpu.SMEM((2,), jnp.int32),
            pltpu.VMEM((2, 2, HALF, rows), jnp.bfloat16),
            pltpu.VMEM((2, 2, rows, HALF), jnp.bfloat16),
            pltpu.VMEM((2, 2, rows, rows), jnp.bfloat16),
            pltpu.SemaphoreType.DMA((16,)),
            pltpu.SemaphoreType.DMA((2,)),
        ],
        compiler_params=pltpu.CompilerParams(vmem_limit_bytes=STAGE_VMEM),
        cost_estimate=pl.CostEstimate(flops=weight, bytes_accessed=weight, transcendentals=0),
        name=name,
    )(*operands)


def cut_kernel(cuts, step, beams, *refs):
    outs, (held, in_sems, out_sems) = refs[: len(cuts)], refs[len(cuts) :]
    pos, many = lax.axis_index("ma"), lax.axis_size("ma")
    inward, outward = [], []
    for (shift, first, height), out in zip(cuts, outs):
        block = beams.at[lax.rem(pos + shift, many)]
        for row in range(0, height, step):
            part = len(inward)
            inward.append(pltpu.make_async_copy(block.at[pl.ds(first + row, step)], held.at[part], in_sems.at[part]))
            outward.append(pltpu.make_async_copy(held.at[part], out.at[pl.ds(row, step)], out_sems.at[part]))
    for copy in inward:
        copy.start()
    for there, back in zip(inward, outward):
        there.wait()
        back.start()
    for copy in outward:
        copy.wait()


def cut_kernel_near(cuts, step, beams, *refs):
    outs, sems = refs[: len(cuts)], refs[len(cuts)]
    pos, many = lax.axis_index("ma"), lax.axis_size("ma")
    copies = []
    for (shift, first, height), out in zip(cuts, outs):
        block = beams.at[lax.rem(pos + shift, many)]
        for row in range(0, height, step):
            source, sem = block.at[pl.ds(first + row, step)], sems.at[len(copies)]
            copies.append(pltpu.make_async_copy(source, out.at[pl.ds(row, step)], sem))
    for copy in copies:
        copy.start()
    for copy in copies:
        copy.wait()


def cut_near(beams, *cuts):
    step = 64
    parts = sum(height for _, _, height in cuts) // step
    return pl.pallas_call(
        functools.partial(cut_kernel_near, cuts, step),
        out_shape=[pltpu.VMEM((height, beams.shape[2]), beams.dtype) for _, _, height in cuts],
        in_specs=[pl.BlockSpec(memory_space=pl.ANY)],
        out_specs=[pl.BlockSpec(memory_space=pltpu.VMEM)] * len(cuts),
        scratch_shapes=[pltpu.SemaphoreType.DMA((parts,))],
        compiler_params=pltpu.CompilerParams(vmem_limit_bytes=VMEM),
        cost_estimate=pl.CostEstimate(flops=10**12, bytes_accessed=1, transcendentals=0),
        name="near",
    )(beams)


def cut_out(beams, *cuts):
    step = 32
    parts = sum(height for _, _, height in cuts) // step
    whole = pl.BlockSpec(memory_space=pl.ANY)
    return pl.pallas_call(
        functools.partial(cut_kernel, cuts, step),
        out_shape=[jax.ShapeDtypeStruct((height, beams.shape[2]), beams.dtype) for _, _, height in cuts],
        in_specs=[whole],
        out_specs=[whole] * len(cuts),
        scratch_shapes=[
            pltpu.VMEM((parts, step, beams.shape[2]), beams.dtype),
            pltpu.SemaphoreType.DMA((parts,)),
            pltpu.SemaphoreType.DMA((parts,)),
        ],
        compiler_params=pltpu.CompilerParams(vmem_limit_bytes=VMEM),
        cost_estimate=pl.CostEstimate(flops=10**12, bytes_accessed=1, transcendentals=0),
        name="cut",
    )(beams)


def along(array, by):
    count = lax.axis_size("ma")
    return lax.ppermute(array, "ma", [(i, (i + by) % count) for i in range(count)])


def beside(array, source, per_band):
    many, groups = lax.axis_size("ma"), lax.axis_size("af")
    pairs = []
    for pos in range(many):
        for group in range(groups):
            channel = (pos + source) % many
            target = group + 1 if channel >= many // 2 else group - 1
            if 0 <= target < groups and target // per_band == group // per_band:
                pairs.append((pos * groups + group, pos * groups + target))
    return lax.ppermute(array, ("ma", "af"), pairs)


def body(beams, spectrum, partners):
    many, _, _, rows, width = beams.shape
    per_band = BAND // many
    beams = beams.reshape(many, rows, width)

    down, up = [None, None], [None, None]
    pos = lax.axis_index("ma")
    down[0], up[0] = (
        lax.dynamic_slice(beams, (lax.rem(pos + shift, many), 0, 0), (1, NEAR, width))[0] for shift in (3, 1)
    )
    again, down[0], up[0] = ORDER((beams, down[0], up[0]))
    down[1], up[1] = cut_near(again, (3, NEAR, rows - NEAR), (1, NEAR, rows - NEAR))
    again, down[1], up[1] = ORDER((beams, down[1], up[1]))
    own, far0, far1 = cut_out(again, (0, 0, rows), (2, 0, FIRST_ROWS), (2, FIRST_ROWS, rows - FIRST_ROWS))
    plan = make_plan(partners, CAPS)

    near1 = [along(part, -1) for part in down]
    near3 = [along(part, 1) for part in up]
    side0 = beside(own, 0, per_band)
    side1 = [beside(near1[0], 1, per_band)]
    side3 = [beside(near3[0], 3, per_band)]
    far0, near1[1], side1[0], side3[0] = ORDER((far0, near1[1], side1[0], side3[0]))
    late0 = along(far0, 2)
    far1, near1[1], near3[1], side0 = ORDER((far1, near1[1], near3[1], side0))
    late1 = along(far1, 2)
    side1.append(beside(near1[1], 1, per_band))
    side3.append(beside(near3[1], 3, per_band))

    ready, fill = (), (0, 1, 2, 3, 6, 7, 8, 9)
    pieces = {(0, 0): beams, (4, 0): side0}
    pieces |= {(1, 0): near1[0], (1, NEAR): near1[1], (3, 0): near3[0], (3, NEAR): near3[1]}
    out, held = run_stage("early", (2,), plan[0], spectrum, pieces, ready, fill, None, None, WEIGHTS[0])

    late0, out = ORDER((late0, out))
    side_first = beside(late0, 2, per_band)
    ready, fill = ready + fill, (4, 10, 11, 14, 15)
    pieces = {(2, 0): late0, (5, 0): side1[0], (5, NEAR): side1[1], (7, 0): side3[0], (7, NEAR): side3[1]}
    out, held = run_stage("middle", (0, 1, 2), plan[1], spectrum, pieces, ready, fill, held, out, WEIGHTS[1])

    late1, out = ORDER((late1, out))
    side_second = beside(late1, 2, per_band)
    side_first, out = ORDER((side_first, out))
    ready, fill = ready + fill, (5, 12)
    pieces = {(2, 0): late0, (2, FIRST_ROWS): late1, (6, 0): side_first}
    out, held = run_stage("late", (0, 1, 2), plan[2], spectrum, pieces, ready, fill, held, out, WEIGHTS[2])

    side_second, out = ORDER((side_second, out))
    ready, fill = ready + fill, (13,)
    pieces = {(6, 0): side_first, (6, FIRST_ROWS): side_second}
    out, held = run_stage("last", (1,), plan[3], spectrum, pieces, ready, fill, held, out, WEIGHTS[3])
    return out[None]


def solution(mesh):
    in_specs = (P(None, "af", "ma", None, None), P("af", None, None), P("af", None))
    out_specs = P("ma", "af", None, None, None, None)
    return jax.shard_map(body, mesh=mesh, in_specs=in_specs, out_specs=out_specs, check_vma=False)
```
